32 devices in a mesh: wide: 8 (over y, x, core), narrow: 4 (over z).
Axes of the slice: x: 2, y: 2, z: 4, core: 2. Of those that a mesh axis runs over, the one named last changes fastest.
Arguments:
- amplitudes: float32 [2, 8, 4, 16, 256, 256], P(None, 'wide', 'narrow'), may hold values from -6 to 6
- low_gate: float32 [2, 256, 256], replicated, may hold values from -0.25 to 0.25
- mid_gate: float32 [2, 256, 256], replicated, may hold values from -0.25 to 0.25
- pair_gates: float32 [3, 2, 4, 4], replicated, may hold values from -2 to 2
Outputs:
- remapped: float32 [2, 8, 4, 16, 256, 256], P(None, 'wide', 'narrow')
The draws below stay inside these ranges and needn't reach their ends.
All inputs are finite; a program needn't handle non-finite values.
Results may differ from the reference program's by a relative error of at most 0.00007.
Values sent between devices are 32-bit elements; how exact they have to be, the bound alone decides.
A program may use at most 128 MiB of HBM per device.

```python
import jax
import jax.numpy as jnp
from jax import lax

GATE = 256
HI = 16
N_WIDE = 8
N_NARROW = 4


def level_of(own_key, extent, cuts, low, top_value):
    gain, own = 1.0, jax.random.fold_in(own_key, 6)
    for dim, shards_of in cuts:
        draws = jnp.exp(jax.random.uniform(jax.random.fold_in(own, dim), (shards_of,), jnp.float32, low / len(cuts), top_value / len(cuts)))
        gain = gain * jnp.repeat(draws, extent[dim] // shards_of).reshape([-1 if axis == dim else 1 for axis in range(len(extent))])
    return gain


def centred(stream_key, extent, scale, most, cuts=(), kind=jnp.bfloat16):
    factor_of = level_of(stream_key, extent, cuts, -0.22, 0.18) if cuts else 1.0
    array = jax.random.normal(stream_key, extent, jnp.float32) * scale * factor_of
    return jnp.minimum(jnp.maximum(array, -most), most).astype(kind)


def setup_inputs(seed: int = 0) -> dict:
    key_list = jax.random.split(jax.random.key(seed), 5)
    amplitudes = centred(key_list[0], (2, N_WIDE, N_NARROW, HI, GATE, GATE), 1.0, 6.0, ((1, 8), (2, 4)), jnp.float32)
    low_gate = centred(key_list[1], (2, GATE, GATE), (2 * GATE) ** -0.5, 0.25, (), jnp.float32)
    mid_gate = centred(key_list[2], (2, GATE, GATE), (2 * GATE) ** -0.5, 0.25, (), jnp.float32)
    pair_gates = centred(key_list[3], (3, 2, 4, 4), 8 ** -0.5, 2.0, (), jnp.float32)
    return dict(amplitudes=amplitudes, low_gate=low_gate, mid_gate=mid_gate, pair_gates=pair_gates)


highest = lax.Precision.HIGHEST


def merged_block(block, low_gate, mid_gate):
    real_part, imag_part = block[0], block[1]
    low_real, low_imag = low_gate[0], low_gate[1]
    first_real = jnp.einsum('nhml,il->nhmi', real_part, low_real, precision=highest) - jnp.einsum('nhml,il->nhmi', imag_part, low_imag, precision=highest)
    first_imag = jnp.einsum('nhml,il->nhmi', real_part, low_imag, precision=highest) + jnp.einsum('nhml,il->nhmi', imag_part, low_real, precision=highest)
    mid_real, mid_imag = mid_gate[0], mid_gate[1]
    second_real = jnp.einsum('nhml,im->nhil', first_real, mid_real, precision=highest) - jnp.einsum('nhml,im->nhil', first_imag, mid_imag, precision=highest)
    second_imag = jnp.einsum('nhml,im->nhil', first_real, mid_imag, precision=highest) + jnp.einsum('nhml,im->nhil', first_imag, mid_real, precision=highest)
    return jnp.stack([second_real, second_imag])


def bit_gate(state, gate, first_axis, first_bit, second_bit):
    shape = state.shape
    second_axis = 3
    new_shape = list(shape[:first_axis]) + [shape[first_axis] >> (first_bit + 1), 2, 1 << first_bit] + list(shape[first_axis + 1:second_axis]) + [shape[second_axis] >> (second_bit + 1), 2, 1 << second_bit] + list(shape[second_axis + 1:])
    first_pos = first_axis + 1
    second_pos = second_axis + 3
    split = jnp.moveaxis(state.reshape(new_shape), (first_pos, second_pos), (1, 2))
    gate_four = gate.reshape(2, 2, 2, 2, 2)
    real_new = jnp.einsum('pqab,ab...->pq...', gate_four[0], split[0], precision=highest) - jnp.einsum('pqab,ab...->pq...', gate_four[1], split[1], precision=highest)
    imag_new = jnp.einsum('pqab,ab...->pq...', gate_four[0], split[1], precision=highest) + jnp.einsum('pqab,ab...->pq...', gate_four[1], split[0], precision=highest)
    joined = jnp.stack([real_new, imag_new])
    return jnp.moveaxis(joined, (1, 2), (first_pos, second_pos)).reshape(shape)


def remap_state(state):
    shape = state.shape
    wide_count = shape[1]
    width = shape[4]
    parts = state.reshape(2, wide_count, shape[2], shape[3], wide_count, width // wide_count, shape[5])
    moved = jnp.transpose(parts, (0, 4, 2, 3, 1, 5, 6))
    return moved.reshape(shape)


def reference(amplitudes, low_gate, mid_gate, pair_gates):
    moved = jnp.moveaxis(amplitudes, 1, 0)

    def one_block(block_now):
        return merged_block(block_now, low_gate, mid_gate)

    mixed = lax.map(one_block, moved)
    state = jnp.moveaxis(mixed, 0, 1)
    state = bit_gate(state, pair_gates[0], 1, 0, 0)
    state = bit_gate(state, pair_gates[1], 1, 2, 1)
    state = bit_gate(state, pair_gates[2], 2, 1, 0)
    return remap_state(state)
```

```python
import functools

import jax
import jax.numpy as jnp
from jax import lax
from jax.experimental import pallas as pl
from jax.experimental.pallas import tpu as pltpu
from jax.sharding import PartitionSpec as P

MESH = pl.DeviceIdType.MESH
CHUNK = 8
highest = lax.Precision.HIGHEST


def merged(x, slot, low, mid):
    gate, lanes = x.shape[2], x.shape[3]
    both = x[slot].reshape(2 * gate, lanes)
    dims = (((1,), (1,)), ((), ()))
    by_real = lax.dot_general(both, low[0], dims, precision=highest, preferred_element_type=jnp.float32)
    by_imag = lax.dot_general(both, low[1], dims, precision=highest, preferred_element_type=jnp.float32)
    first_real = by_real[:gate] - by_imag[gate:]
    first_imag = by_imag[:gate] + by_real[gate:]
    mid_both = mid[...].reshape(2 * gate, gate)
    on_real = jnp.dot(mid_both, first_real, precision=highest, preferred_element_type=jnp.float32)
    on_imag = jnp.dot(mid_both, first_imag, precision=highest, preferred_element_type=jnp.float32)
    x[slot, 0] = on_real[:gate] - on_imag[gate:]
    x[slot, 1] = on_real[gate:] + on_imag[:gate]


def mix(coefs, sources):
    real, imag = None, None
    for (coef_real, coef_imag), (in_real, in_imag) in zip(coefs, sources):
        term_real = coef_real * in_real - coef_imag * in_imag
        term_imag = coef_real * in_imag + coef_imag * in_real
        real = term_real if real is None else real + term_real
        imag = term_imag if imag is None else imag + term_imag
    return real, imag


def pair_on(ref, slots, stride, gates, which):
    coefs = [
        [(gates[which * 32 + row * 4 + col], gates[which * 32 + 16 + row * 4 + col]) for col in range(4)]
        for row in range(4)
    ]
    per = stride // CHUNK

    def step(i, _):
        base = pl.multiple_of((i // per) * (2 * stride) + (i % per) * CHUNK, CHUNK)
        far = pl.multiple_of(base + stride, CHUNK)
        places = [(slots[b], pl.ds(start, CHUNK)) for start in (base, far) for b in range(2)]
        sources = [(ref[s, 0, rows], ref[s, 1, rows]) for s, rows in places]
        results = [mix(coefs[row], sources) for row in range(4)]
        for (s, rows), (real, imag) in zip(places, results):
            ref[s, 0, rows] = real
            ref[s, 1, rows] = imag
        return 0

    lax.fori_loop(0, ref.shape[2] // (2 * CHUNK), step, 0)


def combine(own, far, slots, side, gates):
    def coef(q, a, b):
        at = 64 + (2 * side + q) * 4 + 2 * a + b
        return gates[at], gates[at + 16]

    coefs = [[coef(q, side, 0), coef(q, side, 1), coef(q, 1 - side, 0), coef(q, 1 - side, 1)] for q in range(2)]

    def step(i, _):
        rows = pl.ds(pl.multiple_of(i * CHUNK, CHUNK), CHUNK)
        sources = [(ref[s, 0, rows], ref[s, 1, rows]) for ref in (own, far) for s in slots]
        results = [mix(coefs[q], sources) for q in range(2)]
        for s, (real, imag) in zip(slots, results):
            far[s, 0, rows] = real
            far[s, 1, rows] = imag
        return 0

    lax.fori_loop(0, far.shape[2] // CHUNK, step, 0)


def kernel(n_wide, psi, low, mid, gates, out, x, y, z, load_sem, a2a_send, a2a_recv, raw_send, raw_recv, z_send, z_recv, out_sem):
    heights, gate = psi.shape[1], psi.shape[2]
    pairs = heights // 2
    part = gate // n_wide
    me = lax.axis_index("wide")
    mine = lax.axis_index("narrow")
    side = (mine // 2) % 2
    partner = mine + 2 - 4 * side

    barrier = pltpu.get_barrier_semaphore()

    def greet(d, _):
        pl.semaphore_signal(barrier, inc=1, device_id={"wide": lax.rem(me + d, n_wide)}, device_id_type=MESH)
        return 0

    pl.semaphore_signal(barrier, inc=1, device_id={"narrow": partner}, device_id_type=MESH)
    lax.fori_loop(1, n_wide, greet, 0)

    def load(h):
        return pltpu.make_async_copy(psi.at[:, h], x.at[h], load_sem.at[h])

    def start_load(h, _):
        load(h).start()
        return 0

    lax.fori_loop(0, heights, start_load, 0)
    pl.semaphore_wait(barrier, n_wide)

    def raw(j):
        return pltpu.make_async_remote_copy(
            src_ref=psi.at[:, j], dst_ref=x.at[heights + j], send_sem=raw_send.at[j], recv_sem=raw_recv.at[j],
            device_id={"narrow": partner}, device_id_type=MESH)

    def across(k):
        return pltpu.make_async_remote_copy(
            src_ref=y.at[pl.ds(2 * k, 2)], dst_ref=z.at[pl.ds(2 * k, 2)], send_sem=z_send.at[k], recv_sem=z_recv.at[k],
            device_id={"narrow": partner}, device_id_type=MESH)

    raw(0).start()
    raw(1).start()

    own_rows = pl.ds(pl.multiple_of(me * part, part), part)

    def scatter(slot, dst, dst_slot):
        def send(d, _):
            to = lax.rem(me + d, n_wide)
            pltpu.make_async_remote_copy(
                src_ref=x.at[slot, :, pl.ds(pl.multiple_of(to * part, part), part)],
                dst_ref=dst.at[dst_slot, :, own_rows],
                send_sem=a2a_send.at[slot], recv_sem=a2a_recv.at[slot],
                device_id={"wide": to}, device_id_type=MESH).start()
            return 0

        lax.fori_loop(1, n_wide, send, 0)
        dst[dst_slot, :, own_rows] = x[slot, :, own_rows]

    def all_but_own(ref, slot, sem):
        view = ref.at[slot, :, pl.ds(0, (n_wide - 1) * part)]
        pltpu.make_async_copy(view, view, sem).wait()

    def compute_pair(k):
        def one(h, _):
            load(h).wait()
            merged(x, h, low, mid)
            scatter(h, y, h)
            return 0

        lax.fori_loop(2 * k, 2 * k + 2, one, 0)

    def gathered(k):
        all_but_own(y, 2 * k, a2a_recv.at[2 * k])
        all_but_own(y, 2 * k + 1, a2a_recv.at[2 * k + 1])
        pair_on(y, (2 * k, 2 * k + 1), part, gates, 0)

    compute_pair(1)

    def pipeline(k, _):
        compute_pair(lax.rem(k + 1, pairs))
        gathered(k)
        across(k).start()
        return 0

    lax.fori_loop(1, pairs, pipeline, 0)
    gathered(0)

    def far_one(j, _):
        raw(j).wait_recv()
        merged(x, heights + j, low, mid)
        scatter(heights + j, z, j)
        return 0

    lax.fori_loop(0, 2, far_one, 0)
    all_but_own(z, 0, a2a_recv.at[heights])
    all_but_own(z, 1, a2a_recv.at[heights + 1])
    pair_on(z, (0, 1), part, gates, 0)
    combine(y, z, (0, 1), side, gates)

    def leave(h):
        return pltpu.make_async_copy(z.at[h], out.at[:, h], out_sem.at[h])

    def start_leave(h, _):
        leave(h).start()
        return 0

    def quad(hh, k):
        across(k).wait_recv()
        combine(y, z, (2 * k, 2 * k + 1), side, gates)
        pair_on(z, (4 * hh, 4 * hh + 2), 4 * part, gates, 1)
        pair_on(z, (4 * hh + 1, 4 * hh + 3), 4 * part, gates, 1)
        lax.fori_loop(4 * hh, 4 * hh + 4, start_leave, 0)

    quad(0, 1)

    def finish(hh, _):
        across(2 * hh).wait_recv()
        combine(y, z, (4 * hh, 4 * hh + 1), side, gates)
        quad(hh, 2 * hh + 1)
        return 0

    lax.fori_loop(1, heights // 4, finish, 0)

    def drain(h, _):
        leave(h).wait()
        return 0

    lax.fori_loop(0, heights, drain, 0)

    def sent(slot, _):
        all_but_own(x, slot, a2a_send.at[slot])
        return 0

    lax.fori_loop(0, heights + 2, sent, 0)

    def sent_across(k, _):
        across(k).wait_send()
        return 0

    lax.fori_loop(1, pairs, sent_across, 0)
    raw(0).wait_send()
    raw(1).wait_send()


def body(n_wide, amplitudes, low_gate, mid_gate, pair_gates):
    shape = amplitudes.shape
    psi = amplitudes.reshape(shape[0], shape[3], shape[4], shape[5])
    heights, gate, lanes = psi.shape[1:]
    dma = pltpu.SemaphoreType.DMA
    state = pl.pallas_call(
        functools.partial(kernel, n_wide),
        out_shape=jax.ShapeDtypeStruct(psi.shape, jnp.float32),
        in_specs=[
            pl.BlockSpec(memory_space=pl.ANY),
            pl.BlockSpec(memory_space=pltpu.VMEM),
            pl.BlockSpec(memory_space=pltpu.VMEM),
            pl.BlockSpec(memory_space=pltpu.SMEM),
        ],
        out_specs=pl.BlockSpec(memory_space=pl.ANY),
        scratch_shapes=[
            pltpu.VMEM((heights + 2, 2, gate, lanes), jnp.float32),
            pltpu.VMEM((heights, 2, gate, lanes), jnp.float32),
            pltpu.VMEM((heights, 2, gate, lanes), jnp.float32),
            dma((heights,)),
            dma((heights + 2,)),
            dma((heights + 2,)),
            dma((2,)),
            dma((2,)),
            dma((heights // 2,)),
            dma((heights // 2,)),
            dma((heights,)),
        ],
        compiler_params=pltpu.CompilerParams(
            collective_id=0, has_side_effects=True, vmem_limit_bytes=52 * 2**20
        ),
    )(psi, low_gate, mid_gate, pair_gates.reshape(-1))
    return state.reshape(shape)


def solution(mesh):
    in_specs = (P(None, "wide", "narrow", None, None, None), P(), P(), P())
    out_specs = P(None, "wide", "narrow", None, None, None)
    return jax.shard_map(
        functools.partial(body, mesh.shape["wide"]), mesh=mesh, in_specs=in_specs, out_specs=out_specs, check_vma=False
    )
```

```python
import functools

import jax
import jax.numpy as jnp
from jax import lax
from jax.experimental import pallas as pl
from jax.experimental.pallas import tpu as pltpu
from jax.sharding import PartitionSpec as P

MESH = pl.DeviceIdType.MESH
CHUNK = 8
highest = lax.Precision.HIGHEST


def merged(x, slot, low, mid):
    gate, lanes = x.shape[2], x.shape[3]
    both = x[slot].reshape(2 * gate, lanes)
    dims = (((1,), (1,)), ((), ()))
    by_real = lax.dot_general(both, low[0], dims, precision=highest, preferred_element_type=jnp.float32)
    by_imag = lax.dot_general(both, low[1], dims, precision=highest, preferred_element_type=jnp.float32)
    first_real = by_real[:gate] - by_imag[gate:]
    first_imag = by_imag[:gate] + by_real[gate:]
    mid_both = mid[...].reshape(2 * gate, gate)
    on_real = jnp.dot(mid_both, first_real, precision=highest, preferred_element_type=jnp.float32)
    on_imag = jnp.dot(mid_both, first_imag, precision=highest, preferred_element_type=jnp.float32)
    x[slot, 0] = on_real[:gate] - on_imag[gate:]
    x[slot, 1] = on_real[gate:] + on_imag[:gate]


def mix(coefs, sources):
    real, imag = None, None
    for (coef_real, coef_imag), (in_real, in_imag) in zip(coefs, sources):
        term_real = coef_real * in_real - coef_imag * in_imag
        term_imag = coef_real * in_imag + coef_imag * in_real
        real = term_real if real is None else real + term_real
        imag = term_imag if imag is None else imag + term_imag
    return real, imag


def pair_on(ref, into, slots, stride, gates, which, low_row, span):
    coefs = [
        [(gates[which, 0, row, col], gates[which, 1, row, col]) for col in range(4)]
        for row in range(4)
    ]
    per = span // CHUNK

    def step(i, _):
        base = pl.multiple_of((i // per) * (2 * stride) + low_row + (i % per) * CHUNK, CHUNK)
        far = pl.multiple_of(base + stride, CHUNK)
        places = [(slots[b], pl.ds(start, CHUNK)) for start in (base, far) for b in range(2)]
        sources = [(ref[s, 0, rows], ref[s, 1, rows]) for s, rows in places]
        results = [mix(coefs[row], sources) for row in range(4)]
        for (s, rows), (real, imag) in zip(places, results):
            into(s, rows, real, imag)
        return 0

    lax.fori_loop(0, ref.shape[2] // (2 * stride) * per, step, 0)


def combine(own, far, slots, side, gates, block, low_row, span):
    def coef(q, a, b):
        return gates[2, 0, 2 * side + q, 2 * a + b], gates[2, 1, 2 * side + q, 2 * a + b]

    coefs = [[coef(q, side, 0), coef(q, side, 1), coef(q, 1 - side, 0), coef(q, 1 - side, 1)] for q in range(2)]
    per = span // CHUNK

    def step(i, _):
        rows = pl.ds(pl.multiple_of((i // per) * block + low_row + (i % per) * CHUNK, CHUNK), CHUNK)
        sources = [(ref[s, 0, rows], ref[s, 1, rows]) for ref in (own, far) for s in slots]
        results = [mix(coefs[q], sources) for q in range(2)]
        for s, (real, imag) in zip(slots, results):
            far[s, 0, rows] = real
            far[s, 1, rows] = imag
        return 0

    lax.fori_loop(0, far.shape[2] // block * per, step, 0)


def kernel(n_wide, psi, low_hbm, mid_hbm, gates, out, x, y, z, low, mid, load_sem, gate_sem, a2a_send, a2a_recv, raw_send, raw_recv, z_send, z_recv):
    heights, gate = psi.shape[1], psi.shape[2]
    pairs = heights // 2
    part = gate // n_wide
    block = 4 * part
    last = pairs - 1
    me = lax.axis_index("wide")
    mine = lax.axis_index("narrow")
    side = (mine // 2) % 2
    partner = mine + 2 - 4 * side

    barrier = pltpu.get_barrier_semaphore()

    def greet(d, _):
        pl.semaphore_signal(barrier, inc=1, device_id={"wide": lax.rem(me + d, n_wide)}, device_id_type=MESH)
        return 0

    pl.semaphore_signal(barrier, inc=1, device_id={"narrow": partner}, device_id_type=MESH)
    lax.fori_loop(1, n_wide, greet, 0)

    def load(h):
        return pltpu.make_async_copy(psi.at[:, h], x.at[h], load_sem.at[h])

    def start_load(h, _):
        load(h).start()
        return 0

    fetch_low = pltpu.make_async_copy(low_hbm, low, gate_sem.at[0])
    fetch_mid = pltpu.make_async_copy(mid_hbm, mid, gate_sem.at[1])
    pl.semaphore_wait(barrier, n_wide)

    def raw(j):
        return pltpu.make_async_remote_copy(
            src_ref=psi.at[:, j], dst_ref=x.at[heights + j], send_sem=raw_send.at[j], recv_sem=raw_recv.at[j],
            device_id={"narrow": partner}, device_id_type=MESH)

    def across(k):
        return pltpu.make_async_remote_copy(
            src_ref=y.at[pl.ds(2 * k, 2)], dst_ref=z.at[pl.ds(2 * k, 2)], send_sem=z_send.at[k], recv_sem=z_recv.at[k],
            device_id={"narrow": partner}, device_id_type=MESH)

    def start_piece(j):
        for at in range(j * part, gate, block):
            rows = pl.ds(at, part)
            pltpu.make_async_remote_copy(
                src_ref=y.at[pl.ds(2 * last, 2), :, rows], dst_ref=z.at[pl.ds(2 * last, 2), :, rows],
                send_sem=z_send.at[last + j], recv_sem=z_recv.at[last + j],
                device_id={"narrow": partner}, device_id_type=MESH).start()

    def wait_piece(ref, sem):
        view = ref.at[pl.ds(2 * last, 2), :, pl.ds(0, gate // 4)]
        pltpu.make_async_copy(view, view, sem).wait()

    raw(0).start()
    raw(1).start()
    fetch_low.start()
    fetch_mid.start()
    lax.fori_loop(2, heights, start_load, 0)
    lax.fori_loop(0, 2, start_load, 0)

    own_rows = pl.ds(pl.multiple_of(me * part, part), part)

    def scatter(slot, dst, dst_slot):
        def send(d, _):
            to = lax.rem(me + d, n_wide)
            pltpu.make_async_remote_copy(
                src_ref=x.at[slot, :, pl.ds(pl.multiple_of(to * part, part), part)],
                dst_ref=dst.at[dst_slot, :, own_rows],
                send_sem=a2a_send.at[slot], recv_sem=a2a_recv.at[slot],
                device_id={"wide": to}, device_id_type=MESH).start()
            return 0

        lax.fori_loop(1, n_wide, send, 0)
        dst[dst_slot, :, own_rows] = x[slot, :, own_rows]

    def all_but_own(ref, slot, sem):
        view = ref.at[slot, :, pl.ds(0, (n_wide - 1) * part)]
        pltpu.make_async_copy(view, view, sem).wait()

    def compute_pair(k):
        def one(h, _):
            load(h).wait()
            merged(x, h, low, mid)
            scatter(h, y, h)
            return 0

        lax.fori_loop(2 * k, 2 * k + 2, one, 0)

    def in_place(ref):
        def into(s, rows, real, imag):
            ref[s, 0, rows] = real
            ref[s, 1, rows] = imag

        return into

    def leave(s, rows, real, imag):
        out[0, s, rows] = real
        out[1, s, rows] = imag

    def gathered(k):
        all_but_own(y, 2 * k, a2a_recv.at[2 * k])
        all_but_own(y, 2 * k + 1, a2a_recv.at[2 * k + 1])
        pair_on(y, in_place(y), (2 * k, 2 * k + 1), part, gates, 0, 0, part)

    fetch_low.wait()
    fetch_mid.wait()
    compute_pair(1)

    def pipeline(k, _):
        compute_pair(lax.rem(k + 1, pairs))
        gathered(k)

        @pl.when(k <= 2)
        def _():
            across(k).start()

        return 0

    lax.fori_loop(1, pairs, pipeline, 0)
    gathered(0)

    def far_one(j, _):
        raw(j).wait_recv()
        merged(x, heights + j, low, mid)
        scatter(heights + j, z, j)
        return 0

    lax.fori_loop(0, 2, far_one, 0)
    all_but_own(z, 0, a2a_recv.at[heights])
    all_but_own(z, 1, a2a_recv.at[heights + 1])
    pair_on(z, in_place(z), (0, 1), part, gates, 0, 0, part)
    combine(y, z, (0, 1), side, gates, block, 0, block)

    def arrived(k):
        across(k).wait_recv()

        @pl.when(k + 2 < last)
        def _():
            across(k + 2).start()

    def close(hh, low_row, span):
        for b in range(2):
            pair_on(z, leave, (4 * hh + b, 4 * hh + 2 + b), block, gates, 1, low_row, span)

    def quad(hh, k):
        arrived(k)
        combine(y, z, (2 * k, 2 * k + 1), side, gates, block, 0, block)
        close(hh, 0, block)

    quad(0, 1)
    quads = heights // 4

    def finish(hh, _):
        arrived(2 * hh)
        combine(y, z, (4 * hh, 4 * hh + 1), side, gates, block, 0, block)
        quad(hh, 2 * hh + 1)
        return 0

    lax.fori_loop(1, quads - 1, finish, 0)
    start_piece(0)
    across(last - 1).wait_recv()
    start_piece(1)
    combine(y, z, (2 * last - 2, 2 * last - 1), side, gates, block, 0, block)
    for j in range(4):
        wait_piece(z, z_recv.at[last + j])
        if j < 2:
            start_piece(j + 2)
        combine(y, z, (2 * last, 2 * last + 1), side, gates, block, j * part, part)
        close(quads - 1, j * part, part)

    def sent(slot, _):
        all_but_own(x, slot, a2a_send.at[slot])
        return 0

    lax.fori_loop(0, heights + 2, sent, 0)

    def sent_across(k, _):
        across(k).wait_send()
        return 0

    lax.fori_loop(1, last, sent_across, 0)
    for j in range(4):
        wait_piece(y, z_send.at[last + j])
    raw(0).wait_send()
    raw(1).wait_send()


def body(n_wide, amplitudes, low_gate, mid_gate, pair_gates):
    shape = amplitudes.shape
    psi = amplitudes.reshape(shape[0], shape[3], shape[4], shape[5])
    heights, gate, lanes = psi.shape[1:]
    dma = pltpu.SemaphoreType.DMA
    state = pl.pallas_call(
        functools.partial(kernel, n_wide),
        out_shape=jax.ShapeDtypeStruct(psi.shape, jnp.float32),
        in_specs=[
            pl.BlockSpec(memory_space=pltpu.HBM),
            pl.BlockSpec(memory_space=pltpu.HBM),
            pl.BlockSpec(memory_space=pltpu.HBM),
            pl.BlockSpec(memory_space=pltpu.SMEM),
        ],
        out_specs=pl.BlockSpec(memory_space=pltpu.VMEM),
        scratch_shapes=[
            pltpu.VMEM((heights + 2, 2, gate, lanes), jnp.float32),
            pltpu.VMEM((heights, 2, gate, lanes), jnp.float32),
            pltpu.VMEM((heights, 2, gate, lanes), jnp.float32),
            pltpu.VMEM(low_gate.shape, jnp.float32),
            pltpu.VMEM(mid_gate.shape, jnp.float32),
            dma((heights,)),
            dma((2,)),
            dma((heights + 2,)),
            dma((heights + 2,)),
            dma((2,)),
            dma((2,)),
            dma((heights // 2 + 3,)),
            dma((heights // 2 + 3,)),
        ],
        compiler_params=pltpu.CompilerParams(
            collective_id=0, has_side_effects=True, vmem_limit_bytes=40 * 2**20
        ),
    )(psi, low_gate, mid_gate, pair_gates)
    return state.reshape(shape)


def solution(mesh):
    in_specs = (P(None, "wide", "narrow", None, None, None), P(), P(), P())
    out_specs = P(None, "wide", "narrow", None, None, None)
    return jax.shard_map(
        functools.partial(body, mesh.shape["wide"]), mesh=mesh, in_specs=in_specs, out_specs=out_specs, check_vma=False
    )
```

```python
import functools

import jax
import jax.numpy as jnp
from jax import lax
from jax.experimental import pallas as pl
from jax.experimental.pallas import tpu as pltpu
from jax.sharding import PartitionSpec as P

MESH = pl.DeviceIdType.MESH
CHUNK = 8
highest = lax.Precision.HIGHEST


def merged(x, slot, low, mid):
    gate, lanes = x.shape[2], x.shape[3]
    both = x[slot].reshape(2 * gate, lanes)
    dims = (((1,), (1,)), ((), ()))
    by_real = lax.dot_general(both, low[0], dims, precision=highest, preferred_element_type=jnp.float32)
    by_imag = lax.dot_general(both, low[1], dims, precision=highest, preferred_element_type=jnp.float32)
    first_real = by_real[:gate] - by_imag[gate:]
    first_imag = by_imag[:gate] + by_real[gate:]
    mid_both = mid[...].reshape(2 * gate, gate)
    on_real = jnp.dot(mid_both, first_real, precision=highest, preferred_element_type=jnp.float32)
    on_imag = jnp.dot(mid_both, first_imag, precision=highest, preferred_element_type=jnp.float32)
    x[slot, 0] = on_real[:gate] - on_imag[gate:]
    x[slot, 1] = on_real[gate:] + on_imag[:gate]


def mix(coefs, sources):
    real, imag = None, None
    for (coef_real, coef_imag), (in_real, in_imag) in zip(coefs, sources):
        term_real = coef_real * in_real - coef_imag * in_imag
        term_imag = coef_real * in_imag + coef_imag * in_real
        real = term_real if real is None else real + term_real
        imag = term_imag if imag is None else imag + term_imag
    return real, imag


def pair_on(ref, into, slots, stride, gates, which, low_row, span):
    coefs = [
        [(gates[which, 0, row, col], gates[which, 1, row, col]) for col in range(4)]
        for row in range(4)
    ]
    per = span // CHUNK

    def step(i, _):
        base = pl.multiple_of((i // per) * (2 * stride) + low_row + (i % per) * CHUNK, CHUNK)
        far = pl.multiple_of(base + stride, CHUNK)
        places = [(slots[b], pl.ds(start, CHUNK)) for start in (base, far) for b in range(2)]
        sources = [(ref[s, 0, rows], ref[s, 1, rows]) for s, rows in places]
        results = [mix(coefs[row], sources) for row in range(4)]
        for (s, rows), (real, imag) in zip(places, results):
            into(s, rows, real, imag)
        return 0

    lax.fori_loop(0, ref.shape[2] // (2 * stride) * per, step, 0)


def combine(own, far, slots, side, gates, block, low_row, span):
    def coef(q, a, b):
        return gates[2, 0, 2 * side + q, 2 * a + b], gates[2, 1, 2 * side + q, 2 * a + b]

    coefs = [[coef(q, side, 0), coef(q, side, 1), coef(q, 1 - side, 0), coef(q, 1 - side, 1)] for q in range(2)]
    per = span // CHUNK

    def step(i, _):
        rows = pl.ds(pl.multiple_of((i // per) * block + low_row + (i % per) * CHUNK, CHUNK), CHUNK)
        sources = [(ref[s, 0, rows], ref[s, 1, rows]) for ref in (own, far) for s in slots]
        results = [mix(coefs[q], sources) for q in range(2)]
        for s, (real, imag) in zip(slots, results):
            far[s, 0, rows] = real
            far[s, 1, rows] = imag
        return 0

    lax.fori_loop(0, far.shape[2] // block * per, step, 0)


def kernel(n_wide, psi, low_hbm, mid_hbm, gates_hbm, out, x, y, z, low, mid, gates, load_sem, gate_sem, a2a_send, a2a_recv, raw_send, raw_recv, z_send, z_recv):
    heights, gate = psi.shape[1], psi.shape[2]
    pairs = heights // 2
    part = gate // n_wide
    block = 4 * part
    last = pairs - 1
    me = lax.axis_index("wide")
    mine = lax.axis_index("narrow")
    side = (mine // 2) % 2
    partner = mine + 2 - 4 * side

    barrier = pltpu.get_barrier_semaphore()

    def greet(d, _):
        pl.semaphore_signal(barrier, inc=1, device_id={"wide": lax.rem(me + d, n_wide)}, device_id_type=MESH)
        return 0

    pl.semaphore_signal(barrier, inc=1, device_id={"narrow": partner}, device_id_type=MESH)
    lax.fori_loop(1, n_wide, greet, 0)

    def load(h):
        return pltpu.make_async_copy(psi.at[:, h], x.at[h], load_sem.at[h])

    def start_load(h, _):
        load(h).start()
        return 0

    fetch_low = pltpu.make_async_copy(low_hbm, low, gate_sem.at[0])
    fetch_mid = pltpu.make_async_copy(mid_hbm, mid, gate_sem.at[1])
    fetch_gates = pltpu.make_async_copy(gates_hbm, gates, gate_sem.at[2])
    pl.semaphore_wait(barrier, n_wide)

    def raw(j):
        return pltpu.make_async_remote_copy(
            src_ref=psi.at[:, j], dst_ref=x.at[heights + j], send_sem=raw_send.at[j], recv_sem=raw_recv.at[j],
            device_id={"narrow": partner}, device_id_type=MESH)

    def across(k):
        return pltpu.make_async_remote_copy(
            src_ref=y.at[pl.ds(2 * k, 2)], dst_ref=z.at[pl.ds(2 * k, 2)], send_sem=z_send.at[k], recv_sem=z_recv.at[k],
            device_id={"narrow": partner}, device_id_type=MESH)

    def start_piece(j):
        for at in range(j * part, gate, block):
            rows = pl.ds(at, part)
            pltpu.make_async_remote_copy(
                src_ref=y.at[pl.ds(2 * last, 2), :, rows], dst_ref=z.at[pl.ds(2 * last, 2), :, rows],
                send_sem=z_send.at[last + j], recv_sem=z_recv.at[last + j],
                device_id={"narrow": partner}, device_id_type=MESH).start()

    def wait_piece(ref, sem):
        view = ref.at[pl.ds(2 * last, 2), :, pl.ds(0, gate // 4)]
        pltpu.make_async_copy(view, view, sem).wait()

    raw(0).start()
    raw(1).start()
    fetch_low.start()
    fetch_mid.start()
    fetch_gates.start()
    lax.fori_loop(2, heights, start_load, 0)
    lax.fori_loop(0, 2, start_load, 0)

    own_rows = pl.ds(pl.multiple_of(me * part, part), part)

    def scatter(slot, dst, dst_slot):
        def send(d, _):
            to = lax.rem(me + d, n_wide)
            pltpu.make_async_remote_copy(
                src_ref=x.at[slot, :, pl.ds(pl.multiple_of(to * part, part), part)],
                dst_ref=dst.at[dst_slot, :, own_rows],
                send_sem=a2a_send.at[slot], recv_sem=a2a_recv.at[slot],
                device_id={"wide": to}, device_id_type=MESH).start()
            return 0

        lax.fori_loop(1, n_wide, send, 0)
        dst[dst_slot, :, own_rows] = x[slot, :, own_rows]

    def all_but_own(ref, slot, sem):
        view = ref.at[slot, :, pl.ds(0, (n_wide - 1) * part)]
        pltpu.make_async_copy(view, view, sem).wait()

    def compute_pair(k):
        def one(h, _):
            load(h).wait()
            merged(x, h, low, mid)
            scatter(h, y, h)
            return 0

        lax.fori_loop(2 * k, 2 * k + 2, one, 0)

    def in_place(ref):
        def into(s, rows, real, imag):
            ref[s, 0, rows] = real
            ref[s, 1, rows] = imag

        return into

    def leave(s, rows, real, imag):
        out[0, s, rows] = real
        out[1, s, rows] = imag

    def gathered(k):
        all_but_own(y, 2 * k, a2a_recv.at[2 * k])
        all_but_own(y, 2 * k + 1, a2a_recv.at[2 * k + 1])
        pair_on(y, in_place(y), (2 * k, 2 * k + 1), part, gates, 0, 0, part)

    fetch_low.wait()
    fetch_mid.wait()
    compute_pair(1)
    fetch_gates.wait()

    def pipeline(k, _):
        compute_pair(lax.rem(k + 1, pairs))
        gathered(k)

        @pl.when(k <= 3)
        def _():
            across(k).start()

        return 0

    lax.fori_loop(1, pairs, pipeline, 0)
    gathered(0)

    def far_one(j, _):
        raw(j).wait_recv()
        merged(x, heights + j, low, mid)
        scatter(heights + j, z, j)
        return 0

    lax.fori_loop(0, 2, far_one, 0)
    all_but_own(z, 0, a2a_recv.at[heights])
    all_but_own(z, 1, a2a_recv.at[heights + 1])
    pair_on(z, in_place(z), (0, 1), part, gates, 0, 0, part)
    combine(y, z, (0, 1), side, gates, block, 0, block)

    def arrived(k):
        across(k).wait_recv()

        @pl.when(jnp.logical_and(k + 2 > 3, k + 2 < last))
        def _():
            across(k + 2).start()

    def close(hh, low_row, span):
        for b in range(2):
            pair_on(z, leave, (4 * hh + b, 4 * hh + 2 + b), block, gates, 1, low_row, span)

    def quad(hh, k):
        arrived(k)
        combine(y, z, (2 * k, 2 * k + 1), side, gates, block, 0, block)
        close(hh, 0, block)

    quad(0, 1)
    quads = heights // 4

    def finish(hh, _):
        arrived(2 * hh)
        combine(y, z, (4 * hh, 4 * hh + 1), side, gates, block, 0, block)
        quad(hh, 2 * hh + 1)
        return 0

    lax.fori_loop(1, quads - 1, finish, 0)
    start_piece(0)
    across(last - 1).wait_recv()
    start_piece(1)
    combine(y, z, (2 * last - 2, 2 * last - 1), side, gates, block, 0, block)
    for j in range(4):
        wait_piece(z, z_recv.at[last + j])
        if j < 2:
            start_piece(j + 2)
        combine(y, z, (2 * last, 2 * last + 1), side, gates, block, j * part, part)
        close(quads - 1, j * part, part)

    def sent(slot, _):
        all_but_own(x, slot, a2a_send.at[slot])
        return 0

    lax.fori_loop(0, heights + 2, sent, 0)

    def sent_across(k, _):
        across(k).wait_send()
        return 0

    lax.fori_loop(1, last, sent_across, 0)
    for j in range(4):
        wait_piece(y, z_send.at[last + j])
    raw(0).wait_send()
    raw(1).wait_send()


def body(n_wide, amplitudes, low_gate, mid_gate, pair_gates):
    shape = amplitudes.shape
    psi = amplitudes.reshape(shape[0], shape[3], shape[4], shape[5])
    heights, gate, lanes = psi.shape[1:]
    dma = pltpu.SemaphoreType.DMA
    state = pl.pallas_call(
        functools.partial(kernel, n_wide),
        out_shape=jax.ShapeDtypeStruct(psi.shape, jnp.float32),
        in_specs=[
            pl.BlockSpec(memory_space=pltpu.HBM),
            pl.BlockSpec(memory_space=pltpu.HBM),
            pl.BlockSpec(memory_space=pltpu.HBM),
            pl.BlockSpec(memory_space=pltpu.HBM),
        ],
        out_specs=pl.BlockSpec(memory_space=pltpu.VMEM),
        scratch_shapes=[
            pltpu.VMEM((heights + 2, 2, gate, lanes), jnp.float32),
            pltpu.VMEM((heights, 2, gate, lanes), jnp.float32),
            pltpu.VMEM((heights, 2, gate, lanes), jnp.float32),
            pltpu.VMEM(low_gate.shape, jnp.float32),
            pltpu.VMEM(mid_gate.shape, jnp.float32),
            pltpu.SMEM(pair_gates.shape, jnp.float32),
            dma((heights,)),
            dma((3,)),
            dma((heights + 2,)),
            dma((heights + 2,)),
            dma((2,)),
            dma((2,)),
            dma((heights // 2 + 3,)),
            dma((heights // 2 + 3,)),
        ],
        compiler_params=pltpu.CompilerParams(
            collective_id=0, has_side_effects=True, vmem_limit_bytes=40 * 2**20
        ),
    )(*[pltpu.with_memory_space_constraint(array, pltpu.HBM) for array in (psi, low_gate, mid_gate, pair_gates)])
    return state.reshape(shape)


def solution(mesh):
    in_specs = (P(None, "wide", "narrow", None, None, None), P(), P(), P())
    out_specs = P(None, "wide", "narrow", None, None, None)
    return jax.shard_map(
        functools.partial(body, mesh.shape["wide"]), mesh=mesh, in_specs=in_specs, out_specs=out_specs, check_vma=False
    )
```

```python
import functools

import jax
import jax.numpy as jnp
from jax import lax
from jax.experimental import pallas as pl
from jax.experimental.pallas import tpu as pltpu
from jax.sharding import PartitionSpec as P

MESH = pl.DeviceIdType.MESH
CHUNK = 8
PIECES = 8
highest = lax.Precision.HIGHEST


def merged(x, slot, low, mid):
    gate, lanes = x.shape[2], x.shape[3]
    both = x[slot].reshape(2 * gate, lanes)
    dims = (((1,), (1,)), ((), ()))
    by_real = lax.dot_general(both, low[0], dims, precision=highest, preferred_element_type=jnp.float32)
    by_imag = lax.dot_general(both, low[1], dims, precision=highest, preferred_element_type=jnp.float32)
    first_real = by_real[:gate] - by_imag[gate:]
    first_imag = by_imag[:gate] + by_real[gate:]
    mid_both = mid[...].reshape(2 * gate, gate)
    on_real = jnp.dot(mid_both, first_real, precision=highest, preferred_element_type=jnp.float32)
    on_imag = jnp.dot(mid_both, first_imag, precision=highest, preferred_element_type=jnp.float32)
    x[slot, 0] = on_real[:gate] - on_imag[gate:]
    x[slot, 1] = on_real[gate:] + on_imag[:gate]


def mix(coefs, sources):
    real, imag = None, None
    for (coef_real, coef_imag), (in_real, in_imag) in zip(coefs, sources):
        term_real = coef_real * in_real - coef_imag * in_imag
        term_imag = coef_real * in_imag + coef_imag * in_real
        real = term_real if real is None else real + term_real
        imag = term_imag if imag is None else imag + term_imag
    return real, imag


def pair_on(ref, into, slots, stride, gates, which, low_row, span):
    coefs = [
        [(gates[which, 0, row, col], gates[which, 1, row, col]) for col in range(4)]
        for row in range(4)
    ]
    per = span // CHUNK

    def step(i, _):
        base = pl.multiple_of((i // per) * (2 * stride) + low_row + (i % per) * CHUNK, CHUNK)
        far = pl.multiple_of(base + stride, CHUNK)
        places = [(slots[b], pl.ds(start, CHUNK)) for start in (base, far) for b in range(2)]
        sources = [(ref[s, 0, rows], ref[s, 1, rows]) for s, rows in places]
        results = [mix(coefs[row], sources) for row in range(4)]
        for (s, rows), (real, imag) in zip(places, results):
            into(s, rows, real, imag)
        return 0

    lax.fori_loop(0, ref.shape[2] // (2 * stride) * per, step, 0)


def combine(own, far, slots, side, gates, block, low_row, span):
    def coef(q, a, b):
        return gates[2, 0, 2 * side + q, 2 * a + b], gates[2, 1, 2 * side + q, 2 * a + b]

    coefs = [[coef(q, side, 0), coef(q, side, 1), coef(q, 1 - side, 0), coef(q, 1 - side, 1)] for q in range(2)]
    per = span // CHUNK

    def step(i, _):
        rows = pl.ds(pl.multiple_of((i // per) * block + low_row + (i % per) * CHUNK, CHUNK), CHUNK)
        sources = [(ref[s, 0, rows], ref[s, 1, rows]) for ref in (own, far) for s in slots]
        results = [mix(coefs[q], sources) for q in range(2)]
        for s, (real, imag) in zip(slots, results):
            far[s, 0, rows] = real
            far[s, 1, rows] = imag
        return 0

    lax.fori_loop(0, far.shape[2] // block * per, step, 0)


def kernel(n_wide, n_narrow, psi, low_hbm, mid_hbm, gates_hbm, out, x, y, z, low, mid, gates, load_sem, gate_sem, a2a_send, a2a_recv, raw_send, raw_recv, z_send, z_recv):
    heights, gate = psi.shape[1], psi.shape[2]
    pairs = heights // 2
    part = gate // n_wide
    block = 4 * part
    last = pairs - 1
    span = block // PIECES
    me = lax.axis_index("wide")
    mine = lax.axis_index("narrow")
    side = (mine // 2) % 2
    partner = mine + 2 - 4 * side
    outer = jnp.logical_or(mine == 0, mine == n_narrow - 1)
    inner = jnp.logical_not(outer)

    barrier = pltpu.get_barrier_semaphore()

    def greet(d, _):
        pl.semaphore_signal(barrier, inc=1, device_id={"wide": lax.rem(me + d, n_wide)}, device_id_type=MESH)
        return 0

    pl.semaphore_signal(barrier, inc=1, device_id={"narrow": partner}, device_id_type=MESH)
    lax.fori_loop(1, n_wide, greet, 0)

    def load(h):
        return pltpu.make_async_copy(psi.at[:, h], x.at[h], load_sem.at[h])

    def start_load(h, _):
        load(h).start()
        return 0

    fetch_low = pltpu.make_async_copy(low_hbm, low, gate_sem.at[0])
    fetch_mid = pltpu.make_async_copy(mid_hbm, mid, gate_sem.at[1])
    fetch_gates = pltpu.make_async_copy(gates_hbm, gates, gate_sem.at[2])
    pl.semaphore_wait(barrier, n_wide)

    def raw(j):
        return pltpu.make_async_remote_copy(
            src_ref=psi.at[:, j], dst_ref=x.at[heights + j], send_sem=raw_send.at[j], recv_sem=raw_recv.at[j],
            device_id={"narrow": partner}, device_id_type=MESH)

    def across(k):
        return pltpu.make_async_remote_copy(
            src_ref=y.at[pl.ds(2 * k, 2)], dst_ref=z.at[pl.ds(2 * k, 2)], send_sem=z_send.at[k], recv_sem=z_recv.at[k],
            device_id={"narrow": partner}, device_id_type=MESH)

    def start_piece(j):
        for at in range(j * span, gate, block):
            rows = pl.ds(at, span)
            pltpu.make_async_remote_copy(
                src_ref=y.at[pl.ds(2 * last, 2), :, rows], dst_ref=z.at[pl.ds(2 * last, 2), :, rows],
                send_sem=z_send.at[last + j], recv_sem=z_recv.at[last + j],
                device_id={"narrow": partner}, device_id_type=MESH).start()

    def wait_piece(ref, sem):
        view = ref.at[pl.ds(2 * last, 2), :, pl.ds(0, gate // PIECES)]
        pltpu.make_async_copy(view, view, sem).wait()

    raw(0).start()
    raw(1).start()
    fetch_low.start()
    fetch_mid.start()
    fetch_gates.start()
    lax.fori_loop(2, heights, start_load, 0)
    lax.fori_loop(0, 2, start_load, 0)

    own_rows = pl.ds(pl.multiple_of(me * part, part), part)

    def scatter(slot, dst, dst_slot):
        def send(d, _):
            to = lax.rem(me + d, n_wide)
            pltpu.make_async_remote_copy(
                src_ref=x.at[slot, :, pl.ds(pl.multiple_of(to * part, part), part)],
                dst_ref=dst.at[dst_slot, :, own_rows],
                send_sem=a2a_send.at[slot], recv_sem=a2a_recv.at[slot],
                device_id={"wide": to}, device_id_type=MESH).start()
            return 0

        lax.fori_loop(1, n_wide, send, 0)
        dst[dst_slot, :, own_rows] = x[slot, :, own_rows]

    def all_but_own(ref, slot, sem):
        view = ref.at[slot, :, pl.ds(0, (n_wide - 1) * part)]
        pltpu.make_async_copy(view, view, sem).wait()

    def compute_pair(k):
        def one(h, _):
            load(h).wait()
            merged(x, h, low, mid)
            scatter(h, y, h)
            return 0

        lax.fori_loop(2 * k, 2 * k + 2, one, 0)

    def in_place(ref):
        def into(s, rows, real, imag):
            ref[s, 0, rows] = real
            ref[s, 1, rows] = imag

        return into

    def leave(s, rows, real, imag):
        out[0, s, rows] = real
        out[1, s, rows] = imag

    def gathered(k):
        all_but_own(y, 2 * k, a2a_recv.at[2 * k])
        all_but_own(y, 2 * k + 1, a2a_recv.at[2 * k + 1])
        pair_on(y, in_place(y), (2 * k, 2 * k + 1), part, gates, 0, 0, part)

    fetch_low.wait()
    fetch_mid.wait()
    compute_pair(1)
    fetch_gates.wait()

    def pipeline(k, _):
        compute_pair(lax.rem(k + 1, pairs))
        gathered(k)

        @pl.when(k <= 3)
        def _():
            across(k).start()

        return 0

    lax.fori_loop(1, pairs, pipeline, 0)
    gathered(0)

    def far_one(j, _):
        raw(j).wait_recv()
        merged(x, heights + j, low, mid)
        scatter(heights + j, z, j)
        return 0

    lax.fori_loop(0, 2, far_one, 0)
    all_but_own(z, 0, a2a_recv.at[heights])
    all_but_own(z, 1, a2a_recv.at[heights + 1])
    pair_on(z, in_place(z), (0, 1), part, gates, 0, 0, part)
    combine(y, z, (0, 1), side, gates, block, 0, block)

    def arrived(k):
        across(k).wait_recv()

        @pl.when(jnp.logical_and(k + 2 > 3, k + 2 < last))
        def _():
            across(k + 2).start()

    def close(hh, low_row, span):
        for b in range(2):
            pair_on(z, leave, (4 * hh + b, 4 * hh + 2 + b), block, gates, 1, low_row, span)

    def quad(hh, k):
        arrived(k)
        combine(y, z, (2 * k, 2 * k + 1), side, gates, block, 0, block)
        close(hh, 0, block)

    quad(0, 1)
    quads = heights // 4

    def finish(hh, _):
        arrived(2 * hh)
        combine(y, z, (4 * hh, 4 * hh + 1), side, gates, block, 0, block)
        quad(hh, 2 * hh + 1)
        return 0

    lax.fori_loop(1, quads - 1, finish, 0)
    start_piece(0)

    @pl.when(inner)
    def _():
        start_piece(1)

    def sent(slot, _):
        all_but_own(x, slot, a2a_send.at[slot])
        return 0

    lax.fori_loop(0, heights + 2, sent, 0)

    def sent_across(k, _):
        across(k).wait_send()
        return 0

    raw(0).wait_send()
    raw(1).wait_send()
    across(last - 1).wait_recv()
    combine(y, z, (2 * last - 2, 2 * last - 1), side, gates, block, 0, block)
    for j in range(PIECES):
        wait_piece(z, z_recv.at[last + j])
        if j + 1 < PIECES:
            @pl.when(outer)
            def _():
                start_piece(j + 1)

        if j + 2 < PIECES:
            @pl.when(inner)
            def _():
                start_piece(j + 2)

        if j == PIECES - 2:
            lax.fori_loop(1, last, sent_across, 0)
        combine(y, z, (2 * last, 2 * last + 1), side, gates, block, j * span, span)
        close(quads - 1, j * span, span)

    for j in range(PIECES):
        wait_piece(y, z_send.at[last + j])


def write(state, out, sems):
    copies = [
        pltpu.make_async_copy(state.at[c, h], out.at[c, h], sems.at[c, h])
        for c in range(state.shape[0]) for h in range(state.shape[1])
    ]
    for copy in copies:
        copy.start()
    for copy in copies:
        copy.wait()


def body(n_wide, n_narrow, amplitudes, low_gate, mid_gate, pair_gates):
    shape = amplitudes.shape
    psi = amplitudes.reshape(shape[0], shape[3], shape[4], shape[5])
    heights, gate, lanes = psi.shape[1:]
    dma = pltpu.SemaphoreType.DMA
    state = pl.pallas_call(
        functools.partial(kernel, n_wide, n_narrow),
        out_shape=jax.ShapeDtypeStruct(psi.shape, jnp.float32),
        in_specs=[
            pl.BlockSpec(memory_space=pltpu.HBM),
            pl.BlockSpec(memory_space=pltpu.HBM),
            pl.BlockSpec(memory_space=pltpu.HBM),
            pl.BlockSpec(memory_space=pltpu.HBM),
        ],
        out_specs=pl.BlockSpec(memory_space=pltpu.VMEM),
        scratch_shapes=[
            pltpu.VMEM((heights + 2, 2, gate, lanes), jnp.float32),
            pltpu.VMEM((heights, 2, gate, lanes), jnp.float32),
            pltpu.VMEM((heights, 2, gate, lanes), jnp.float32),
            pltpu.VMEM(low_gate.shape, jnp.float32),
            pltpu.VMEM(mid_gate.shape, jnp.float32),
            pltpu.SMEM(pair_gates.shape, jnp.float32),
            dma((heights,)),
            dma((3,)),
            dma((heights + 2,)),
            dma((heights + 2,)),
            dma((2,)),
            dma((2,)),
            dma((heights // 2 - 1 + PIECES,)),
            dma((heights // 2 - 1 + PIECES,)),
        ],
        compiler_params=pltpu.CompilerParams(
            collective_id=0, has_side_effects=True, vmem_limit_bytes=40 * 2**20
        ),
    )(*[pltpu.with_memory_space_constraint(array, pltpu.HBM) for array in (psi, low_gate, mid_gate, pair_gates)])
    result = pl.pallas_call(
        write,
        out_shape=jax.ShapeDtypeStruct(psi.shape, jnp.float32),
        in_specs=[pl.BlockSpec(memory_space=pltpu.VMEM)],
        out_specs=pl.BlockSpec(memory_space=pltpu.HBM),
        scratch_shapes=[dma(psi.shape[:2])],
        compiler_params=pltpu.CompilerParams(vmem_limit_bytes=16 * 2**20),
    )(state)
    return result.reshape(shape)


def solution(mesh):
    in_specs = (P(None, "wide", "narrow", None, None, None), P(), P(), P())
    out_specs = P(None, "wide", "narrow", None, None, None)
    return jax.shard_map(
        functools.partial(body, mesh.shape["wide"], mesh.shape["narrow"]), mesh=mesh, in_specs=in_specs, out_specs=out_specs, check_vma=False
    )
```

```python
import functools

import jax
import jax.numpy as jnp
from jax import lax
from jax.experimental import pallas as pl
from jax.experimental.pallas import tpu as pltpu
from jax.sharding import PartitionSpec as P

MESH = pl.DeviceIdType.MESH
CHUNK = 8
PIECES = 8
AHEAD = 4
highest = lax.Precision.HIGHEST


def merged(x, slot, low, mid):
    gate, lanes = x.shape[2], x.shape[3]
    both = x[slot].reshape(2 * gate, lanes)
    dims = (((1,), (1,)), ((), ()))
    by_real = lax.dot_general(both, low[0], dims, precision=highest, preferred_element_type=jnp.float32)
    by_imag = lax.dot_general(both, low[1], dims, precision=highest, preferred_element_type=jnp.float32)
    first_real = by_real[:gate] - by_imag[gate:]
    first_imag = by_imag[:gate] + by_real[gate:]
    mid_both = mid[...].reshape(2 * gate, gate)
    on_real = jnp.dot(mid_both, first_real, precision=highest, preferred_element_type=jnp.float32)
    on_imag = jnp.dot(mid_both, first_imag, precision=highest, preferred_element_type=jnp.float32)
    x[slot, 0] = on_real[:gate] - on_imag[gate:]
    x[slot, 1] = on_real[gate:] + on_imag[:gate]


def mix(coefs, sources):
    real, imag = None, None
    for (coef_real, coef_imag), (in_real, in_imag) in zip(coefs, sources):
        term_real = coef_real * in_real - coef_imag * in_imag
        term_imag = coef_real * in_imag + coef_imag * in_real
        real = term_real if real is None else real + term_real
        imag = term_imag if imag is None else imag + term_imag
    return real, imag


def pair_on(ref, into, slots, stride, gates, which, low_row, span):
    coefs = [
        [(gates[which, 0, row, col], gates[which, 1, row, col]) for col in range(4)]
        for row in range(4)
    ]
    per = span // CHUNK

    def step(i, _):
        base = pl.multiple_of((i // per) * (2 * stride) + low_row + (i % per) * CHUNK, CHUNK)
        far = pl.multiple_of(base + stride, CHUNK)
        places = [(slots[b], pl.ds(start, CHUNK)) for start in (base, far) for b in range(2)]
        sources = [(ref[s, 0, rows], ref[s, 1, rows]) for s, rows in places]
        results = [mix(coefs[row], sources) for row in range(4)]
        for (s, rows), (real, imag) in zip(places, results):
            into(s, rows, real, imag)
        return 0

    lax.fori_loop(0, ref.shape[2] // (2 * stride) * per, step, 0)


def combine(own, far, slots, side, gates, block, low_row, span):
    def coef(q, a, b):
        return gates[2, 0, 2 * side + q, 2 * a + b], gates[2, 1, 2 * side + q, 2 * a + b]

    coefs = [[coef(q, side, 0), coef(q, side, 1), coef(q, 1 - side, 0), coef(q, 1 - side, 1)] for q in range(2)]
    per = span // CHUNK

    def step(i, _):
        rows = pl.ds(pl.multiple_of((i // per) * block + low_row + (i % per) * CHUNK, CHUNK), CHUNK)
        sources = [(ref[s, 0, rows], ref[s, 1, rows]) for ref in (own, far) for s in slots]
        results = [mix(coefs[q], sources) for q in range(2)]
        for s, (real, imag) in zip(slots, results):
            far[s, 0, rows] = real
            far[s, 1, rows] = imag
        return 0

    lax.fori_loop(0, far.shape[2] // block * per, step, 0)


def kernel(n_wide, psi, low_hbm, mid_hbm, gates_hbm, out, x, y, z, low, mid, gates, load_sem, gate_sem, a2a_send, a2a_recv, raw_send, raw_recv, z_send, z_recv):
    heights, gate = psi.shape[1], psi.shape[2]
    pairs = heights // 2
    part = gate // n_wide
    block = 4 * part
    last = pairs - 1
    span = block // PIECES
    me = lax.axis_index("wide")
    mine = lax.axis_index("narrow")
    side = (mine // 2) % 2
    partner = mine + 2 - 4 * side

    barrier = pltpu.get_barrier_semaphore()

    def greet(d, _):
        pl.semaphore_signal(barrier, inc=1, device_id={"wide": lax.rem(me + d, n_wide)}, device_id_type=MESH)
        return 0

    pl.semaphore_signal(barrier, inc=1, device_id={"narrow": partner}, device_id_type=MESH)
    lax.fori_loop(1, n_wide, greet, 0)

    def load(h):
        return pltpu.make_async_copy(psi.at[:, h], x.at[h], load_sem.at[h])

    def start_load(h, _):
        load(h).start()
        return 0

    fetch_low = pltpu.make_async_copy(low_hbm, low, gate_sem.at[0])
    fetch_mid = pltpu.make_async_copy(mid_hbm, mid, gate_sem.at[1])
    fetch_gates = pltpu.make_async_copy(gates_hbm, gates, gate_sem.at[2])
    pl.semaphore_wait(barrier, n_wide)

    def raw(j):
        return pltpu.make_async_remote_copy(
            src_ref=psi.at[:, j], dst_ref=x.at[heights + j], send_sem=raw_send.at[j], recv_sem=raw_recv.at[j],
            device_id={"narrow": partner}, device_id_type=MESH)

    def across(k):
        return pltpu.make_async_remote_copy(
            src_ref=y.at[pl.ds(2 * k, 2)], dst_ref=z.at[pl.ds(2 * k, 2)], send_sem=z_send.at[k], recv_sem=z_recv.at[k],
            device_id={"narrow": partner}, device_id_type=MESH)

    def start_piece(j):
        for at in range(j * span, gate, block):
            rows = pl.ds(at, span)
            pltpu.make_async_remote_copy(
                src_ref=y.at[pl.ds(2 * last, 2), :, rows], dst_ref=z.at[pl.ds(2 * last, 2), :, rows],
                send_sem=z_send.at[last + j], recv_sem=z_recv.at[last + j],
                device_id={"narrow": partner}, device_id_type=MESH).start()

    def wait_piece(ref, sem):
        view = ref.at[pl.ds(2 * last, 2), :, pl.ds(0, gate // PIECES)]
        pltpu.make_async_copy(view, view, sem).wait()

    raw(0).start()
    raw(1).start()
    fetch_low.start()
    fetch_mid.start()
    fetch_gates.start()
    lax.fori_loop(2, heights, start_load, 0)
    lax.fori_loop(0, 2, start_load, 0)

    own_rows = pl.ds(pl.multiple_of(me * part, part), part)

    def scatter(slot, dst, dst_slot):
        def send(d, _):
            to = lax.rem(me + d, n_wide)
            pltpu.make_async_remote_copy(
                src_ref=x.at[slot, :, pl.ds(pl.multiple_of(to * part, part), part)],
                dst_ref=dst.at[dst_slot, :, own_rows],
                send_sem=a2a_send.at[slot], recv_sem=a2a_recv.at[slot],
                device_id={"wide": to}, device_id_type=MESH).start()
            return 0

        lax.fori_loop(1, n_wide, send, 0)
        dst[dst_slot, :, own_rows] = x[slot, :, own_rows]

    def all_but_own(ref, slot, sem):
        view = ref.at[slot, :, pl.ds(0, (n_wide - 1) * part)]
        pltpu.make_async_copy(view, view, sem).wait()

    def compute_pair(k):
        def one(h, _):
            load(h).wait()
            merged(x, h, low, mid)
            scatter(h, y, h)
            return 0

        lax.fori_loop(2 * k, 2 * k + 2, one, 0)

    def in_place(ref):
        def into(s, rows, real, imag):
            ref[s, 0, rows] = real
            ref[s, 1, rows] = imag

        return into

    def leave(s, rows, real, imag):
        out[0, s, rows] = real
        out[1, s, rows] = imag

    def gathered(k):
        all_but_own(y, 2 * k, a2a_recv.at[2 * k])
        all_but_own(y, 2 * k + 1, a2a_recv.at[2 * k + 1])
        pair_on(y, in_place(y), (2 * k, 2 * k + 1), part, gates, 0, 0, part)

    fetch_low.wait()
    fetch_mid.wait()
    compute_pair(1)
    fetch_gates.wait()

    def pipeline(k, _):
        compute_pair(lax.rem(k + 1, pairs))
        gathered(k)

        @pl.when(k <= 3)
        def _():
            across(k).start()

        return 0

    lax.fori_loop(1, pairs, pipeline, 0)
    gathered(0)

    def far_one(j, _):
        raw(j).wait_recv()
        merged(x, heights + j, low, mid)
        scatter(heights + j, z, j)
        return 0

    lax.fori_loop(0, 2, far_one, 0)
    all_but_own(z, 0, a2a_recv.at[heights])
    all_but_own(z, 1, a2a_recv.at[heights + 1])
    pair_on(z, in_place(z), (0, 1), part, gates, 0, 0, part)
    combine(y, z, (0, 1), side, gates, block, 0, block)

    def arrived(k):
        across(k).wait_recv()

        @pl.when(jnp.logical_and(k + 2 > 3, k + 2 < last))
        def _():
            across(k + 2).start()

    def close(hh, low_row, span):
        for b in range(2):
            pair_on(z, leave, (4 * hh + b, 4 * hh + 2 + b), block, gates, 1, low_row, span)

    def quad(hh, k):
        arrived(k)
        combine(y, z, (2 * k, 2 * k + 1), side, gates, block, 0, block)
        close(hh, 0, block)

    quad(0, 1)
    quads = heights // 4

    def finish(hh, _):
        arrived(2 * hh)
        combine(y, z, (4 * hh, 4 * hh + 1), side, gates, block, 0, block)
        quad(hh, 2 * hh + 1)
        return 0

    lax.fori_loop(1, quads - 1, finish, 0)
    for j in range(AHEAD):
        start_piece(j)

    def sent(slot, _):
        all_but_own(x, slot, a2a_send.at[slot])
        return 0

    lax.fori_loop(0, heights + 2, sent, 0)

    def sent_across(k, _):
        across(k).wait_send()
        return 0

    raw(0).wait_send()
    raw(1).wait_send()
    across(last - 1).wait_recv()
    combine(y, z, (2 * last - 2, 2 * last - 1), side, gates, block, 0, block)
    for j in range(PIECES):
        wait_piece(z, z_recv.at[last + j])
        if j + AHEAD < PIECES:
            start_piece(j + AHEAD)
        if j == PIECES - 2:
            lax.fori_loop(1, last, sent_across, 0)
        combine(y, z, (2 * last, 2 * last + 1), side, gates, block, j * span, span)
        close(quads - 1, j * span, span)

    for j in range(PIECES):
        wait_piece(y, z_send.at[last + j])


def body(n_wide, amplitudes, low_gate, mid_gate, pair_gates):
    shape = amplitudes.shape
    psi = amplitudes.reshape(shape[0], shape[3], shape[4], shape[5])
    heights, gate, lanes = psi.shape[1:]
    dma = pltpu.SemaphoreType.DMA
    state = pl.pallas_call(
        functools.partial(kernel, n_wide),
        out_shape=jax.ShapeDtypeStruct(psi.shape, jnp.float32),
        in_specs=[
            pl.BlockSpec(memory_space=pltpu.HBM),
            pl.BlockSpec(memory_space=pltpu.HBM),
            pl.BlockSpec(memory_space=pltpu.HBM),
            pl.BlockSpec(memory_space=pltpu.HBM),
        ],
        out_specs=pl.BlockSpec(memory_space=pltpu.VMEM),
        scratch_shapes=[
            pltpu.VMEM((heights + 2, 2, gate, lanes), jnp.float32),
            pltpu.VMEM((heights, 2, gate, lanes), jnp.float32),
            pltpu.VMEM((heights, 2, gate, lanes), jnp.float32),
            pltpu.VMEM(low_gate.shape, jnp.float32),
            pltpu.VMEM(mid_gate.shape, jnp.float32),
            pltpu.SMEM(pair_gates.shape, jnp.float32),
            dma((heights,)),
            dma((3,)),
            dma((heights + 2,)),
            dma((heights + 2,)),
            dma((2,)),
            dma((2,)),
            dma((heights // 2 - 1 + PIECES,)),
            dma((heights // 2 - 1 + PIECES,)),
        ],
        compiler_params=pltpu.CompilerParams(
            collective_id=0, has_side_effects=True, vmem_limit_bytes=40 * 2**20
        ),
    )(*[pltpu.with_memory_space_constraint(array, pltpu.HBM) for array in (psi, low_gate, mid_gate, pair_gates)])
    return state.reshape(shape)


def solution(mesh):
    in_specs = (P(None, "wide", "narrow", None, None, None), P(), P(), P())
    out_specs = P(None, "wide", "narrow", None, None, None)
    return jax.shard_map(
        functools.partial(body, mesh.shape["wide"]), mesh=mesh, in_specs=in_specs, out_specs=out_specs, check_vma=False
    )
```

```python
import functools

import jax
import jax.numpy as jnp
from jax import lax
from jax.experimental import pallas as pl
from jax.experimental.pallas import tpu as pltpu
from jax.sharding import PartitionSpec as P

MESH = pl.DeviceIdType.MESH
CHUNK = 8
PIECES = 8
OUTER_AHEAD = 3
INNER_AHEAD = 5
highest = lax.Precision.HIGHEST


def merged(x, slot, low, mid):
    gate, lanes = x.shape[2], x.shape[3]
    both = x[slot].reshape(2 * gate, lanes)
    dims = (((1,), (1,)), ((), ()))
    by_real = lax.dot_general(both, low[0], dims, precision=highest, preferred_element_type=jnp.float32)
    by_imag = lax.dot_general(both, low[1], dims, precision=highest, preferred_element_type=jnp.float32)
    first_real = by_real[:gate] - by_imag[gate:]
    first_imag = by_imag[:gate] + by_real[gate:]
    mid_both = mid[...].reshape(2 * gate, gate)
    on_real = jnp.dot(mid_both, first_real, precision=highest, preferred_element_type=jnp.float32)
    on_imag = jnp.dot(mid_both, first_imag, precision=highest, preferred_element_type=jnp.float32)
    x[slot, 0] = on_real[:gate] - on_imag[gate:]
    x[slot, 1] = on_real[gate:] + on_imag[:gate]


def mix(coefs, sources):
    real, imag = None, None
    for (coef_real, coef_imag), (in_real, in_imag) in zip(coefs, sources):
        term_real = coef_real * in_real - coef_imag * in_imag
        term_imag = coef_real * in_imag + coef_imag * in_real
        real = term_real if real is None else real + term_real
        imag = term_imag if imag is None else imag + term_imag
    return real, imag


def pair_on(ref, into, slots, stride, gates, which, low_row, span):
    coefs = [
        [(gates[which, 0, row, col], gates[which, 1, row, col]) for col in range(4)]
        for row in range(4)
    ]
    per = span // CHUNK

    def step(i, _):
        base = pl.multiple_of((i // per) * (2 * stride) + low_row + (i % per) * CHUNK, CHUNK)
        far = pl.multiple_of(base + stride, CHUNK)
        places = [(slots[b], pl.ds(start, CHUNK)) for start in (base, far) for b in range(2)]
        sources = [(ref[s, 0, rows], ref[s, 1, rows]) for s, rows in places]
        results = [mix(coefs[row], sources) for row in range(4)]
        for (s, rows), (real, imag) in zip(places, results):
            into(s, rows, real, imag)
        return 0

    lax.fori_loop(0, ref.shape[2] // (2 * stride) * per, step, 0)


def combine(own, far, slots, side, gates, block, low_row, span):
    def coef(q, a, b):
        return gates[2, 0, 2 * side + q, 2 * a + b], gates[2, 1, 2 * side + q, 2 * a + b]

    coefs = [[coef(q, side, 0), coef(q, side, 1), coef(q, 1 - side, 0), coef(q, 1 - side, 1)] for q in range(2)]
    per = span // CHUNK

    def step(i, _):
        rows = pl.ds(pl.multiple_of((i // per) * block + low_row + (i % per) * CHUNK, CHUNK), CHUNK)
        sources = [(ref[s, 0, rows], ref[s, 1, rows]) for ref in (own, far) for s in slots]
        results = [mix(coefs[q], sources) for q in range(2)]
        for s, (real, imag) in zip(slots, results):
            far[s, 0, rows] = real
            far[s, 1, rows] = imag
        return 0

    lax.fori_loop(0, far.shape[2] // block * per, step, 0)


def kernel(n_wide, n_narrow, psi, low_hbm, mid_hbm, gates_hbm, out, x, y, z, low, mid, gates, load_sem, gate_sem, a2a_send, a2a_recv, raw_send, raw_recv, z_send, z_recv):
    heights, gate = psi.shape[1], psi.shape[2]
    pairs = heights // 2
    part = gate // n_wide
    block = 4 * part
    last = pairs - 1
    span = block // PIECES
    me = lax.axis_index("wide")
    mine = lax.axis_index("narrow")
    side = (mine // 2) % 2
    partner = mine + 2 - 4 * side
    outer = jnp.logical_or(mine == 0, mine == n_narrow - 1)
    inner = jnp.logical_not(outer)

    barrier = pltpu.get_barrier_semaphore()

    def greet(d, _):
        pl.semaphore_signal(barrier, inc=1, device_id={"wide": lax.rem(me + d, n_wide)}, device_id_type=MESH)
        return 0

    pl.semaphore_signal(barrier, inc=1, device_id={"narrow": partner}, device_id_type=MESH)
    lax.fori_loop(1, n_wide, greet, 0)

    def load(h):
        return pltpu.make_async_copy(psi.at[:, h], x.at[h], load_sem.at[h])

    def start_load(h, _):
        load(h).start()
        return 0

    fetch_low = pltpu.make_async_copy(low_hbm, low, gate_sem.at[0])
    fetch_mid = pltpu.make_async_copy(mid_hbm, mid, gate_sem.at[1])
    fetch_gates = pltpu.make_async_copy(gates_hbm, gates, gate_sem.at[2])
    pl.semaphore_wait(barrier, n_wide)

    def raw(j):
        return pltpu.make_async_remote_copy(
            src_ref=psi.at[:, j], dst_ref=x.at[heights + j], send_sem=raw_send.at[j], recv_sem=raw_recv.at[j],
            device_id={"narrow": partner}, device_id_type=MESH)

    def across(k):
        return pltpu.make_async_remote_copy(
            src_ref=y.at[pl.ds(2 * k, 2)], dst_ref=z.at[pl.ds(2 * k, 2)], send_sem=z_send.at[k], recv_sem=z_recv.at[k],
            device_id={"narrow": partner}, device_id_type=MESH)

    def start_piece(j):
        for at in range(j * span, gate, block):
            rows = pl.ds(at, span)
            pltpu.make_async_remote_copy(
                src_ref=y.at[pl.ds(2 * last, 2), :, rows], dst_ref=z.at[pl.ds(2 * last, 2), :, rows],
                send_sem=z_send.at[last + j], recv_sem=z_recv.at[last + j],
                device_id={"narrow": partner}, device_id_type=MESH).start()

    def wait_piece(ref, sem):
        view = ref.at[pl.ds(2 * last, 2), :, pl.ds(0, gate // PIECES)]
        pltpu.make_async_copy(view, view, sem).wait()

    raw(0).start()
    raw(1).start()
    fetch_low.start()
    fetch_mid.start()
    fetch_gates.start()
    lax.fori_loop(2, heights, start_load, 0)
    lax.fori_loop(0, 2, start_load, 0)

    own_rows = pl.ds(pl.multiple_of(me * part, part), part)

    def scatter(slot, dst, dst_slot):
        def send(d, _):
            to = lax.rem(me + d, n_wide)
            pltpu.make_async_remote_copy(
                src_ref=x.at[slot, :, pl.ds(pl.multiple_of(to * part, part), part)],
                dst_ref=dst.at[dst_slot, :, own_rows],
                send_sem=a2a_send.at[slot], recv_sem=a2a_recv.at[slot],
                device_id={"wide": to}, device_id_type=MESH).start()
            return 0

        lax.fori_loop(1, n_wide, send, 0)
        dst[dst_slot, :, own_rows] = x[slot, :, own_rows]

    def all_but_own(ref, slot, sem):
        view = ref.at[slot, :, pl.ds(0, (n_wide - 1) * part)]
        pltpu.make_async_copy(view, view, sem).wait()

    def compute_pair(k):
        def one(h, _):
            load(h).wait()
            merged(x, h, low, mid)
            scatter(h, y, h)
            return 0

        lax.fori_loop(2 * k, 2 * k + 2, one, 0)

    def in_place(ref):
        def into(s, rows, real, imag):
            ref[s, 0, rows] = real
            ref[s, 1, rows] = imag

        return into

    def leave(s, rows, real, imag):
        out[0, s, rows] = real
        out[1, s, rows] = imag

    def gathered(k):
        all_but_own(y, 2 * k, a2a_recv.at[2 * k])
        all_but_own(y, 2 * k + 1, a2a_recv.at[2 * k + 1])
        pair_on(y, in_place(y), (2 * k, 2 * k + 1), part, gates, 0, 0, part)

    fetch_low.wait()
    fetch_mid.wait()
    compute_pair(1)
    fetch_gates.wait()

    def pipeline(k, _):
        compute_pair(lax.rem(k + 1, pairs))
        gathered(k)

        @pl.when(k <= 3)
        def _():
            across(k).start()

        return 0

    lax.fori_loop(1, pairs, pipeline, 0)
    gathered(0)

    def far_one(j, _):
        raw(j).wait_recv()
        merged(x, heights + j, low, mid)
        scatter(heights + j, z, j)
        return 0

    lax.fori_loop(0, 2, far_one, 0)
    all_but_own(z, 0, a2a_recv.at[heights])
    all_but_own(z, 1, a2a_recv.at[heights + 1])
    pair_on(z, in_place(z), (0, 1), part, gates, 0, 0, part)
    combine(y, z, (0, 1), side, gates, block, 0, block)

    def arrived(k):
        across(k).wait_recv()

        @pl.when(jnp.logical_and(k + 2 > 3, k + 2 < last))
        def _():
            across(k + 2).start()

    def close(hh, low_row, span):
        for b in range(2):
            pair_on(z, leave, (4 * hh + b, 4 * hh + 2 + b), block, gates, 1, low_row, span)

    def quad(hh, k):
        arrived(k)
        combine(y, z, (2 * k, 2 * k + 1), side, gates, block, 0, block)
        close(hh, 0, block)

    quad(0, 1)
    quads = heights // 4

    def finish(hh, _):
        arrived(2 * hh)
        combine(y, z, (4 * hh, 4 * hh + 1), side, gates, block, 0, block)
        quad(hh, 2 * hh + 1)
        return 0

    lax.fori_loop(1, quads - 1, finish, 0)
    for j in range(INNER_AHEAD):
        if j < OUTER_AHEAD:
            start_piece(j)
        else:
            pl.when(inner)(functools.partial(start_piece, j))

    def sent(slot, _):
        all_but_own(x, slot, a2a_send.at[slot])
        return 0

    lax.fori_loop(0, heights + 2, sent, 0)

    def sent_across(k, _):
        across(k).wait_send()
        return 0

    raw(0).wait_send()
    raw(1).wait_send()
    across(last - 1).wait_recv()
    combine(y, z, (2 * last - 2, 2 * last - 1), side, gates, block, 0, block)
    for j in range(PIECES):
        wait_piece(z, z_recv.at[last + j])
        if j + OUTER_AHEAD < PIECES:
            pl.when(outer)(functools.partial(start_piece, j + OUTER_AHEAD))
        if j + INNER_AHEAD < PIECES:
            pl.when(inner)(functools.partial(start_piece, j + INNER_AHEAD))
        if j == PIECES - 2:
            lax.fori_loop(1, last, sent_across, 0)
        combine(y, z, (2 * last, 2 * last + 1), side, gates, block, j * span, span)
        close(quads - 1, j * span, span)

    for j in range(PIECES):
        wait_piece(y, z_send.at[last + j])


def body(n_wide, n_narrow, amplitudes, low_gate, mid_gate, pair_gates):
    shape = amplitudes.shape
    psi = amplitudes.reshape(shape[0], shape[3], shape[4], shape[5])
    heights, gate, lanes = psi.shape[1:]
    dma = pltpu.SemaphoreType.DMA
    state = pl.pallas_call(
        functools.partial(kernel, n_wide, n_narrow),
        out_shape=jax.ShapeDtypeStruct(psi.shape, jnp.float32),
        in_specs=[
            pl.BlockSpec(memory_space=pltpu.HBM),
            pl.BlockSpec(memory_space=pltpu.HBM),
            pl.BlockSpec(memory_space=pltpu.HBM),
            pl.BlockSpec(memory_space=pltpu.HBM),
        ],
        out_specs=pl.BlockSpec(memory_space=pltpu.VMEM),
        scratch_shapes=[
            pltpu.VMEM((heights + 2, 2, gate, lanes), jnp.float32),
            pltpu.VMEM((heights, 2, gate, lanes), jnp.float32),
            pltpu.VMEM((heights, 2, gate, lanes), jnp.float32),
            pltpu.VMEM(low_gate.shape, jnp.float32),
            pltpu.VMEM(mid_gate.shape, jnp.float32),
            pltpu.SMEM(pair_gates.shape, jnp.float32),
            dma((heights,)),
            dma((3,)),
            dma((heights + 2,)),
            dma((heights + 2,)),
            dma((2,)),
            dma((2,)),
            dma((heights // 2 - 1 + PIECES,)),
            dma((heights // 2 - 1 + PIECES,)),
        ],
        compiler_params=pltpu.CompilerParams(
            collective_id=0, has_side_effects=True, vmem_limit_bytes=40 * 2**20
        ),
    )(*[pltpu.with_memory_space_constraint(array, pltpu.HBM) for array in (psi, low_gate, mid_gate, pair_gates)])
    return state.reshape(shape)


def solution(mesh):
    in_specs = (P(None, "wide", "narrow", None, None, None), P(), P(), P())
    out_specs = P(None, "wide", "narrow", None, None, None)
    return jax.shard_map(
        functools.partial(body, mesh.shape["wide"], mesh.shape["narrow"]), mesh=mesh, in_specs=in_specs, out_specs=out_specs, check_vma=False
    )
```
